32 devices in a mesh: gx: 8 (over y, x, core), gy: 4 (over z).
Axes of the slice: x: 2, y: 2, z: 4, core: 2. Of those that a mesh axis runs over, the one named last changes fastest.
Arguments:
- velocity: float32 [3, 64, 64, 128], P(None, 'gx', 'gy'), may hold values from -6 to 6
- marker_force: float32 [3, 4096, 128], P(None, ('gx', 'gy')), may hold values from -6 to 6
- marker_cell: int32 [4096, 128], P(('gx', 'gy')), may hold values from 0 to 16383
- block_brick: int32 [4096, 1], P(('gx', 'gy')), may hold values from 0 to 31; in each aligned block of 128 rows (0 to 127, 128 to 255, ...) at most 8 rows name the same one
Outputs:
- velocity_new: float32 [3, 64, 64, 128], P(None, 'gx', 'gy')
- marker_velocity: float32 [3, 4096, 128], P(None, ('gx', 'gy'))
The draws below stay inside these ranges and needn't reach their ends.
Inputs may be any that keep to these rules, and one draw needn't show every extreme that they name: `block_brick`: among the 128 blocks of one device no brick is named by more than 8 blocks, and some device names some brick exactly 8 times.
All inputs are finite; a program needn't handle non-finite values.
Results may differ from the reference program's by a relative error of at most 0.0003.
Values sent between devices are 32-bit elements; how exact they have to be, the bound alone decides.
A program may use at most 128 MiB of HBM per device.

```python
import math
import jax
import jax.numpy as jnp
import numpy as np
from jax import lax

CX = 8
CY = 16
CZ = 128
MB = 128
MARK = 128
SWEEPS = 4
STEPS = 2
CAP = 8
NX = 64
NY = 64
BLOCKS = 4096
N_GY = 4
DEVICES = 32


def place_ends(array, rng, least, largest):
    index_at = [jax.random.randint(jax.random.fold_in(rng, axis), (), 0, length) for axis, length in enumerate(array.shape)]
    widest = array.shape.index(max(array.shape))
    next_to = index_at[:widest] + [(index_at[widest] + 1) % array.shape[widest]] + index_at[widest + 1:]
    return array.at[tuple(index_at)].set(least).at[tuple(next_to)].set(largest)


def steps_of(own_key, shape, cuts, low, top_value):
    level, own = 1.0, jax.random.fold_in(own_key, 6)
    for dim, shards_of in cuts:
        steps = jnp.exp(jax.random.uniform(jax.random.fold_in(own, dim), (shards_of,), jnp.float32, low / len(cuts), top_value / len(cuts)))
        level = level * jnp.repeat(steps, shape[dim] // shards_of).reshape([-1 if axis == dim else 1 for axis in range(len(shape))])
    return level


def assign_block(rng, own, number, rows, amount, top, most, lean):
    order = jax.random.permutation(rng, amount)
    packed, common = portions_of(amount, rows * top, most, lean, True), portions_of(amount, rows * top, most, lean, False)
    places = jnp.arange(amount)

    def named(sizes, turn):
        used = int((sizes > 0).sum())
        fixed = max(1, used // 4)
        passed = fixed + (places - fixed + turn * (used - fixed)) % max(1, amount - fixed)
        return jnp.zeros((amount,), jnp.int32).at[order[jnp.where(places < fixed, places, passed)]].set(jnp.asarray(sizes, jnp.int32))

    sizes = jnp.where(number % 4 == 0, named(packed, number // 4), named(common, number - number // 4 - 1))
    mixed = jax.random.permutation(jax.random.fold_in(own, 3), amount)
    donor, sink = mixed[0:amount // 2 * 2:2], mixed[1:amount // 2 * 2:2]
    margin = jnp.minimum(sizes[donor] - 1, most - sizes[sink]) // 2
    margin = jnp.where((donor == order[0]) | (sink == order[0]) | (sizes[sink] == 0), 0, jnp.maximum(margin, 0))
    passed = jax.random.randint(jax.random.fold_in(own, 4), (amount // 2,), 0, 1 << 20) % (margin + 1)
    sizes = sizes.at[donor].add(-passed).at[sink].add(passed)
    members = jnp.searchsorted(jnp.cumsum(sizes), jnp.arange(rows * top), side="right").astype(jnp.int32)
    grid = members.reshape(top, rows).T
    grid = grid[jax.random.permutation(jax.random.fold_in(own, 1), rows)]
    turn = jax.random.randint(jax.random.fold_in(own, 2), (rows, 1), 0, top)
    return jnp.take_along_axis(grid, (jnp.arange(top)[None, :] + turn) % top, axis=1)


def portions_of(amount, total, reach, lean, full):
    weights = [(1 << 20) // math.isqrt(rank ** lean) + 1 for rank in range(1, amount + 1)]
    largest = reach if full else min(reach, max(-(-total // amount), total * weights[0] // sum(weights)))
    least = 1 if total - largest >= amount - 1 else 0
    holding, rest = [largest] + [least] * (amount - 1), total - largest - least * (amount - 1)
    while rest > 0:
        candidates = [i for i in range(1, amount) if holding[i] < largest] or [i for i in range(1, amount) if holding[i] < reach]
        mass, remaining = sum([weights[i] for i in candidates]), rest
        for i in candidates:
            addition = min(reach - holding[i], max(1, remaining * weights[i] // mass), rest)
            holding[i] = holding[i] + addition
            rest = rest - addition
    return np.array(holding)


def bell_draw(rng, shape, deviation, bound, shards=(), kind=jnp.bfloat16):
    level = steps_of(rng, shape, shards, -0.22, 0.18) if shards else 1.0
    drawn = jax.random.normal(rng, shape, jnp.float32) * deviation * level
    return jnp.minimum(jnp.maximum(drawn, -bound), bound).astype(kind)


def setup_inputs(seed: int = 0) -> dict:
    keys = jax.random.split(jax.random.key(seed), 5)
    velocity = bell_draw(keys[0], (3, NX, NY, CZ), 1.0, 6.0, ((1, 8), (2, 4)), jnp.float32)
    marker_force = bell_draw(keys[1], (3, BLOCKS, MARK), 1.0, 6.0, ((1, 32),), jnp.float32)
    marker_cell = place_ends(jax.random.randint(keys[2], (BLOCKS, MARK), 0, CX * CY * CZ), jax.random.fold_in(keys[2], 1), 0, (CX * CY * CZ) - 1).astype(jnp.int32)
    block_brick_keys = jax.random.split(jax.random.fold_in(keys[3], 1), BLOCKS // MB)
    block_brick_turns = jax.random.permutation(jax.random.fold_in(keys[3], 3), BLOCKS // MB)
    block_brick = jax.vmap(lambda own, number: assign_block(jax.random.fold_in(keys[3], 2), own, number, MB, DEVICES, 1, CAP, 2))(block_brick_keys, block_brick_turns).reshape((BLOCKS, 1))
    return dict(velocity=velocity, marker_force=marker_force, marker_cell=marker_cell, block_brick=block_brick)


time_step = 0.5
viscosity = 0.2
stiffness = 1.0


def neighbours(grid_field):
    padded = jnp.pad(grid_field, [(0, 0)] * (grid_field.ndim - 3) + [(1, 1)] * 3)
    total_sum = padded[..., 2:, 1:-1, 1:-1] + padded[..., :-2, 1:-1, 1:-1]
    total_sum = total_sum + padded[..., 1:-1, 2:, 1:-1] + padded[..., 1:-1, :-2, 1:-1]
    return total_sum + padded[..., 1:-1, 1:-1, 2:] + padded[..., 1:-1, 1:-1, :-2]


def central(grid_field, direction):
    position = grid_field.ndim - 3 + direction
    widths = [(0, 0)] * grid_field.ndim
    widths[position] = (1, 1)
    padded = jnp.pad(grid_field, widths)
    length = padded.shape[position]
    forward = lax.slice_in_dim(padded, 2, length, axis=position)
    behind = lax.slice_in_dim(padded, 0, length - 2, axis=position)
    return 0.5 * (forward - behind)


def reference(velocity, marker_force, marker_cell, block_brick):
    size_x, size_y, size_z = velocity.shape[1], velocity.shape[2], velocity.shape[3]
    dest_brick = block_brick[:, 0]
    brick_x = dest_brick // N_GY
    brick_y = dest_brick % N_GY
    cell_x = marker_cell // (CY * CZ)
    cell_y = (marker_cell // CZ) % CY
    cell_z = marker_cell % CZ
    global_x = brick_x[:, None] * CX + cell_x
    global_y = brick_y[:, None] * CY + cell_y
    flat_cell = ((global_x * size_y + global_y) * size_z + cell_z).reshape(-1).astype(jnp.int32)
    force_now = marker_force.reshape(3, -1)
    current = velocity
    picked = force_now
    for step_number in range(STEPS):
        spread = jnp.zeros((3, size_x * size_y * size_z), current.dtype).at[:, flat_cell].add(force_now)
        spread = spread.reshape(current.shape)
        provisional = current + time_step * (viscosity * (neighbours(current) - 6.0 * current) + spread)
        source = (central(provisional[0], 0) + central(provisional[1], 1) + central(provisional[2], 2)) / time_step
        pressure = jnp.zeros_like(source)
        for sweep_number in range(SWEEPS):
            pressure = (neighbours(pressure) - source) / 6.0
        slope = jnp.stack([central(pressure, 0), central(pressure, 1), central(pressure, 2)])
        current = provisional - time_step * slope
        picked = current.reshape(3, -1)[:, flat_cell]
        if step_number + 1 < STEPS:
            force_now = force_now - stiffness * picked
    return current, picked.reshape(marker_force.shape)
```

```python
import functools

import jax
import jax.numpy as jnp
from jax import lax
from jax.experimental import pallas as pl
from jax.experimental.pallas import tpu as pltpu
from jax.sharding import PartitionSpec as P

SWEEPS = 4
STEPS = 2
MESH = pl.DeviceIdType.MESH

time_step = 0.5
viscosity = 0.2
stiffness = 1.0

HALO_X = SWEEPS + 2
HALO_Y = 8

BF = jnp.bfloat16
VMEM = pl.BlockSpec(memory_space=pltpu.VMEM)
SMEM = pl.BlockSpec(memory_space=pltpu.SMEM)
DIRECTIONS = [(i, j) for i in (-1, 0, 1) for j in (-1, 0, 1) if (i, j) != (0, 0)]


def pack_kernel(devices, cap, brick_ref, force_ref, cell_ref, out_ref, dest_ref, rank_ref, seen):
    blocks, width = cell_ref.shape
    out_ref[:, : 3 * cap, :] = jnp.zeros((devices, 3 * cap, width), jnp.float32)
    out_ref[:, 3 * cap :, :] = jnp.full((devices, cap, width), -1.0, jnp.float32)

    def clear(i, carry):
        seen[i] = 0
        return carry

    lax.fori_loop(0, devices, clear, 0)

    def place(b, carry):
        dest = brick_ref[b]
        rank = seen[dest]
        seen[dest] = rank + 1
        dest_ref[b] = dest
        rank_ref[b] = rank
        for c in range(3):
            out_ref[dest, pl.ds(c * cap + rank, 1), :] = force_ref[c, pl.ds(b, 1), :]
        out_ref[dest, pl.ds(3 * cap + rank, 1), :] = cell_ref[pl.ds(b, 1), :].astype(jnp.float32)
        return carry

    lax.fori_loop(0, blocks, place, 0, unroll=4)


def peer_of(me, k, devices, n_gy):
    peer = lax.rem(me + k, devices)
    return (peer // n_gy, lax.rem(peer, n_gy))


def exchange_kernel(devices, n_gy, src_ref, dst_ref, send_sem, recv_sem, own_sem):
    me = lax.axis_index("gx") * n_gy + lax.axis_index("gy")
    barrier = pltpu.get_barrier_semaphore()

    def greet(k, carry):
        pl.semaphore_signal(
            barrier, inc=1, device_id=peer_of(me, k, devices, n_gy), device_id_type=MESH
        )
        return carry

    lax.fori_loop(1, devices, greet, 0)
    own = pltpu.make_async_copy(src_ref.at[me], dst_ref.at[me], own_sem)
    own.start()
    pl.semaphore_wait(barrier, devices - 1)

    def copy_to(k):
        return pltpu.make_async_remote_copy(
            src_ref=src_ref.at[lax.rem(me + k, devices)],
            dst_ref=dst_ref.at[me],
            send_sem=send_sem.at[k],
            recv_sem=recv_sem.at[k],
            device_id=peer_of(me, k, devices, n_gy),
            device_id_type=MESH,
        )

    def copy_from(k):
        sender = lax.rem(me + devices - k, devices)
        return pltpu.make_async_remote_copy(
            src_ref=src_ref.at[sender],
            dst_ref=dst_ref.at[sender],
            send_sem=send_sem.at[k],
            recv_sem=recv_sem.at[k],
            device_id=peer_of(me, k, devices, n_gy),
            device_id_type=MESH,
        )

    def begin(k, carry):
        copy_to(k).start()
        return carry

    def finish(k, carry):
        copy_from(k).wait_recv()
        return carry

    def drain(k, carry):
        copy_to(k).wait_send()
        return carry

    lax.fori_loop(1, devices, begin, 0)
    lax.fori_loop(1, devices, finish, 0)
    lax.fori_loop(1, devices, drain, 0)
    own.wait()


def exchange(sent, devices, n_gy, number):
    return pl.pallas_call(
        functools.partial(exchange_kernel, devices, n_gy),
        out_shape=jax.ShapeDtypeStruct(sent.shape, sent.dtype),
        in_specs=[VMEM],
        out_specs=VMEM,
        scratch_shapes=[
            pltpu.SemaphoreType.DMA((devices,)),
            pltpu.SemaphoreType.DMA((devices,)),
            pltpu.SemaphoreType.DMA,
        ],
        compiler_params=pltpu.CompilerParams(
            collective_id=number, has_side_effects=True, vmem_limit_bytes=32 << 20
        ),
    )(sent)


def cell_parts(cells, half, depth):
    row = cells // depth
    short = jnp.where(cells < 0, -1, lax.rem(row, half))
    long = (row // half) * depth + lax.rem(cells, depth)
    return short.astype(jnp.float32), long.astype(jnp.float32)


def tall(row):
    return jnp.broadcast_to(row, (16, row.shape[1])).astype(BF)


def one_hot_mask(row, size):
    shape = (size // 16, 16, row.shape[1])
    index = lax.broadcasted_iota(jnp.int32, shape, 0) * 16 + lax.broadcasted_iota(jnp.int32, shape, 1)
    return index.astype(jnp.float32).astype(BF) == tall(row)[None]


def spread_kernel(cap, group, half, depth, in_ref, out_ref, acc):
    count = in_ref.shape[0]
    width = in_ref.shape[2]
    acc[...] = jnp.zeros_like(acc)

    def one(i, carry):
        lefts, rights = [], []
        for g in range(group):
            block = in_ref[i * group + g]
            short, long = cell_parts(block[3 * cap :].astype(jnp.int32), half, depth)
            high = block[: 3 * cap].astype(BF).astype(jnp.float32)
            low = block[: 3 * cap] - high
            for e in range(cap):
                mask = one_hot_mask(short[e : e + 1], half)
                zero = jnp.zeros((16, width), BF)
                one_ = jnp.ones((16, width), BF)
                pieces = []
                for part in (high, low):
                    for c in range(3):
                        value = tall(part[c * cap + e : c * cap + e + 1])
                        pieces.append(jnp.where(mask, value[None], zero[None]).reshape(half, width))
                pieces.append(jnp.where(mask, one_[None], zero[None]).reshape(half, width))
                lefts.append(jnp.concatenate(pieces, axis=0))
                spot = one_hot_mask(long[e : e + 1], 2 * depth)
                rights.append(jnp.where(spot, one_[None], zero[None]).reshape(2 * depth, width))
        left = jnp.concatenate(lefts, axis=1)
        right = jnp.concatenate(rights, axis=1)
        acc[...] += lax.dot_general(
            left, right, (((1,), (1,)), ((), ())), preferred_element_type=jnp.float32
        )
        return carry

    lax.fori_loop(0, count // group, one, 0)
    for c in range(4):
        if c < 3:
            total = acc[c * half : (c + 1) * half] + acc[(3 + c) * half : (4 + c) * half]
        else:
            total = acc[6 * half : 7 * half]
        out_ref[c, :half, :] = total[:, :depth]
        out_ref[c, half:, :] = total[:, depth:]


def pick_kernel(cap, group, half, depth, in_ref, flow_ref, out_ref):
    count = in_ref.shape[0]
    width = in_ref.shape[2]
    table = jnp.concatenate(
        [jnp.concatenate([flow_ref[c, :half], flow_ref[c, half:]], axis=1) for c in range(3)], axis=0
    )
    high = table.astype(BF)
    low = (table - high.astype(jnp.float32)).astype(BF)
    table = jnp.concatenate([high, low], axis=0)
    index = lax.broadcasted_iota(jnp.int32, (half, width), 0).astype(jnp.float32)

    def one(i, carry):
        rights, shorts = [], []
        for g in range(group):
            cells = in_ref[i * group + g, 3 * cap :, :].astype(jnp.int32)
            short, long = cell_parts(cells, half, depth)
            for e in range(cap):
                spot = one_hot_mask(long[e : e + 1], 2 * depth)
                one_ = jnp.ones((16, width), BF)[None]
                zero = jnp.zeros((16, width), BF)[None]
                rights.append(jnp.where(spot, one_, zero).reshape(2 * depth, width))
                shorts.append(short[e : e + 1])
        both = jnp.dot(table, jnp.concatenate(rights, axis=1), preferred_element_type=jnp.float32)
        for g in range(group):
            rows = []
            for c in range(3):
                for e in range(cap):
                    n = g * cap + e
                    cut = both[:, n * width : (n + 1) * width]
                    value = cut[c * half : (c + 1) * half] + cut[(3 + c) * half : (4 + c) * half]
                    mask = index == shorts[n]
                    rows.append(jnp.sum(jnp.where(mask, value, 0.0), axis=0, keepdims=True))
            out_ref[i * group + g] = jnp.concatenate(rows, axis=0)
        return carry

    lax.fori_loop(0, count // group, one, 0)


def unpack_kernel(cap, dest_ref, rank_ref, in_ref, out_ref):
    blocks = out_ref.shape[1]

    def take(b, carry):
        dest = dest_ref[b]
        rank = rank_ref[b]
        for c in range(3):
            out_ref[c, pl.ds(b, 1), :] = in_ref[dest, pl.ds(c * cap + rank, 1), :]
        return carry

    lax.fori_loop(0, blocks, take, 0, unroll=4)


def flow_kernel(n_gx, n_gy, flow_ref, spread_ref, out_ref, wide, moved, later, send_sem, recv_sem):
    size_x, size_y, depth = flow_ref.shape[1:]
    gx, gy = lax.axis_index("gx"), lax.axis_index("gy")

    def exists(dx, dy):
        x, y = gx + dx, gy + dy
        return (x >= 0) & (x < n_gx) & (y >= 0) & (y < n_gy)

    def cut(d, size, halo):
        if d == 0:
            return (0, size), (halo, size)
        if d > 0:
            return (size - halo, halo), (0, halo)
        return (0, halo), (halo + size, halo)

    def copy(turn, number, src, first, fields):
        dx, dy = DIRECTIONS[number]
        (sx, nx), (tx, _) = cut(dx, size_x, HALO_X)
        (sy, ny), (ty, _) = cut(dy, size_y, HALO_Y)
        target = later if turn else wide
        return pltpu.make_async_remote_copy(
            src_ref=src.at[:, pl.ds(sx, nx), pl.ds(sy, ny), :],
            dst_ref=target.at[pl.ds(first, fields), pl.ds(tx, nx), pl.ds(ty, ny), :],
            send_sem=send_sem.at[turn, number],
            recv_sem=recv_sem.at[turn, number],
            device_id=(gx + dx, gy + dy),
            device_id_type=MESH,
        )

    barrier = pltpu.get_barrier_semaphore()
    for dx, dy in DIRECTIONS:

        @pl.when(exists(dx, dy))
        def _():
            pl.semaphore_signal(barrier, inc=1, device_id=(gx + dx, gy + dy), device_id_type=MESH)

    inner = (slice(HALO_X, HALO_X + size_x), slice(HALO_Y, HALO_Y + size_y))
    moved[:3] = flow_ref[...]
    moved[3:] = spread_ref[...].reshape(4, size_x, size_y, depth)
    span_x = 1 + exists(-1, 0).astype(jnp.int32) + exists(1, 0).astype(jnp.int32)
    span_y = 1 + exists(0, -1).astype(jnp.int32) + exists(0, 1).astype(jnp.int32)
    pl.semaphore_wait(barrier, span_x * span_y - 1)

    def run_exchange(turn, src, target, fields):
        for number, (dx, dy) in enumerate(DIRECTIONS):

            @pl.when(exists(dx, dy))
            def _():
                copy(turn, number, src, 0, fields).start()

            @pl.when(jnp.logical_not(exists(-dx, -dy)))
            def _():
                _, (tx, nx) = cut(dx, size_x, HALO_X)
                _, (ty, ny) = cut(dy, size_y, HALO_Y)
                target[:, tx : tx + nx, ty : ty + ny, :] = jnp.zeros(
                    (fields, nx, ny, depth), jnp.float32
                )

        target[:, inner[0], inner[1], :] = src[...]
        for number, (dx, dy) in enumerate(DIRECTIONS):

            @pl.when(exists(-dx, -dy))
            def _():
                copy(turn, number, src, 0, fields).wait_recv()

        for number, (dx, dy) in enumerate(DIRECTIONS):

            @pl.when(exists(dx, dy))
            def _():
                copy(turn, number, src, 0, fields).wait_send()

    wide_x, wide_y = size_x + 2 * HALO_X, size_y + 2 * HALO_Y
    place_x = lax.broadcasted_iota(jnp.int32, (wide_x, wide_y, depth), 0) + (gx * size_x - HALO_X)
    place_y = lax.broadcasted_iota(jnp.int32, (wide_x, wide_y, depth), 1) + (gy * size_y - HALO_Y)
    keep = (
        (place_x >= 0) & (place_x < n_gx * size_x) & (place_y >= 0) & (place_y < n_gy * size_y)
    ).astype(jnp.float32)
    level = lax.broadcasted_iota(jnp.int32, (1, wide_y, depth), 2)
    not_first = (level > 0).astype(jnp.float32)
    not_last = (level < depth - 1).astype(jnp.float32)

    def up_y(v):
        return pltpu.roll(v, wide_y - 1, 1)

    def down_y(v):
        return pltpu.roll(v, 1, 1)

    def up_z(v):
        return pltpu.roll(v, depth - 1, 2) * not_last

    def down_z(v):
        return pltpu.roll(v, 1, 2) * not_first

    def around(v):
        mid = v[1:-1]
        return (v[2:] + v[:-2]) + (up_y(mid) + down_y(mid)) + (up_z(mid) + down_z(mid))

    def advance(flow, force):
        provisional = []
        for c in range(3):
            mid = flow[c][1:-1]
            stepped = mid + time_step * (viscosity * (around(flow[c]) - 6.0 * mid) + force[c][1:-1])
            provisional.append(stepped * keep[1:-1])
        p0, p1, p2 = provisional
        source = (
            0.5 * (p0[2:] - p0[:-2])
            + 0.5 * (up_y(p1[1:-1]) - down_y(p1[1:-1]))
            + 0.5 * (up_z(p2[1:-1]) - down_z(p2[1:-1]))
        ) / time_step
        pressure = -source * keep[2:-2] / 6.0
        for sweep in range(1, SWEEPS):
            edge = sweep + 2
            pressure = (around(pressure) - source[sweep:-sweep]) * keep[edge:-edge] / 6.0
        mid = pressure[1:-1]
        slopes = (
            0.5 * (pressure[2:] - pressure[:-2]),
            0.5 * (up_y(mid) - down_y(mid)),
            0.5 * (up_z(mid) - down_z(mid)),
        )
        far = HALO_X - 1
        return [(provisional[c][far:-far] - time_step * slopes[c])[:, inner[1], :] for c in range(3)]

    run_exchange(0, moved, wide, 7)
    result = advance([wide[c] for c in range(3)], [wide[3 + c] for c in range(3)])
    for c in range(3):
        out_ref[c] = result[c]
    for turn in range(1, STEPS):
        run_exchange(turn, out_ref, later, 3)
        flow = [later[c] for c in range(3)]
        force = [wide[3 + c] - stiffness * wide[6] * flow[c] for c in range(3)]
        result = advance(flow, force)
        for c in range(3):
            out_ref[c] = result[c]


def body(n_gx, n_gy, velocity, marker_force, marker_cell, block_brick):
    devices = n_gx * n_gy
    blocks, width = marker_cell.shape
    size_x, size_y, depth = velocity.shape[1:]
    cap = 2 * blocks // devices
    rows = size_x * size_y
    half = rows // 2
    group = max(1, 8 // cap)
    sent, dest, rank = pl.pallas_call(
        functools.partial(pack_kernel, devices, cap),
        out_shape=(
            jax.ShapeDtypeStruct((devices, 4 * cap, width), jnp.float32),
            jax.ShapeDtypeStruct((blocks,), jnp.int32),
            jax.ShapeDtypeStruct((blocks,), jnp.int32),
        ),
        in_specs=[SMEM, VMEM, VMEM],
        out_specs=(VMEM, SMEM, SMEM),
        scratch_shapes=[pltpu.SMEM((devices,), jnp.int32)],
    )(block_brick.reshape(blocks), marker_force, marker_cell)
    held = exchange(sent, devices, n_gy, 0)
    spread = pl.pallas_call(
        functools.partial(spread_kernel, cap, group, half, depth),
        out_shape=jax.ShapeDtypeStruct((4, rows, depth), jnp.float32),
        in_specs=[VMEM],
        out_specs=VMEM,
        scratch_shapes=[pltpu.VMEM((7 * half, 2 * depth), jnp.float32)],
        compiler_params=pltpu.CompilerParams(vmem_limit_bytes=40 << 20),
    )(held)
    wide = (size_x + 2 * HALO_X, size_y + 2 * HALO_Y, depth)
    current = pl.pallas_call(
        functools.partial(flow_kernel, n_gx, n_gy),
        out_shape=jax.ShapeDtypeStruct(velocity.shape, jnp.float32),
        in_specs=[VMEM, VMEM],
        out_specs=VMEM,
        scratch_shapes=[
            pltpu.VMEM((7,) + wide, jnp.float32),
            pltpu.VMEM((7, size_x, size_y, depth), jnp.float32),
            pltpu.VMEM((3,) + wide, jnp.float32),
            pltpu.SemaphoreType.DMA((STEPS, 8)),
            pltpu.SemaphoreType.DMA((STEPS, 8)),
        ],
        compiler_params=pltpu.CompilerParams(
            collective_id=1, has_side_effects=True, vmem_limit_bytes=40 << 20
        ),
    )(velocity, spread)
    picked = pl.pallas_call(
        functools.partial(pick_kernel, cap, group, half, depth),
        out_shape=jax.ShapeDtypeStruct((devices, 3 * cap, width), jnp.float32),
        in_specs=[VMEM, VMEM],
        out_specs=VMEM,
        compiler_params=pltpu.CompilerParams(vmem_limit_bytes=40 << 20),
    )(held, current.reshape(3, rows, depth))
    returned = exchange(picked, devices, n_gy, 2)
    marker_velocity = pl.pallas_call(
        functools.partial(unpack_kernel, cap),
        out_shape=jax.ShapeDtypeStruct((3, blocks, width), jnp.float32),
        in_specs=[SMEM, SMEM, VMEM],
        out_specs=VMEM,
    )(dest, rank, returned)
    return current, marker_velocity


def solution(mesh):
    n_gx, n_gy = mesh.shape["gx"], mesh.shape["gy"]
    return jax.shard_map(
        functools.partial(body, n_gx, n_gy),
        mesh=mesh,
        in_specs=(
            P(None, "gx", "gy", None),
            P(None, ("gx", "gy"), None),
            P(("gx", "gy"), None),
            P(("gx", "gy"), None),
        ),
        out_specs=(P(None, "gx", "gy", None), P(None, ("gx", "gy"), None)),
        check_vma=False,
    )
```

```python
import functools

import jax
import jax.numpy as jnp
from jax import lax
from jax.experimental import pallas as pl
from jax.experimental.pallas import tpu as pltpu
from jax.sharding import PartitionSpec as P

SWEEPS = 4
STEPS = 2
MESH = pl.DeviceIdType.MESH

time_step = 0.5
viscosity = 0.2
stiffness = 1.0

HALO_X = SWEEPS + 2
HALO_Y = 8

BF = jnp.bfloat16
VMEM = pl.BlockSpec(memory_space=pltpu.VMEM)
SMEM = pl.BlockSpec(memory_space=pltpu.SMEM)
DIRECTIONS = [(i, j) for i in (-1, 0, 1) for j in (-1, 0, 1) if (i, j) != (0, 0)]


def pack_kernel(devices, cap, brick_ref, force_ref, cell_ref, out_ref, dest_ref, rank_ref, seen):
    blocks, width = cell_ref.shape
    out_ref[:, : 3 * cap, :] = jnp.zeros((devices, 3 * cap, width), jnp.float32)
    out_ref[:, 3 * cap :, :] = jnp.full((devices, cap, width), -1.0, jnp.float32)

    def clear(i, carry):
        seen[i] = 0
        return carry

    lax.fori_loop(0, devices, clear, 0)

    def place(b, carry):
        dest = brick_ref[b]
        rank = seen[dest]
        seen[dest] = rank + 1
        dest_ref[b] = dest
        rank_ref[b] = rank
        for c in range(3):
            out_ref[dest, pl.ds(c * cap + rank, 1), :] = force_ref[c, pl.ds(b, 1), :]
        out_ref[dest, pl.ds(3 * cap + rank, 1), :] = cell_ref[pl.ds(b, 1), :].astype(jnp.float32)
        return carry

    lax.fori_loop(0, blocks, place, 0, unroll=4)


def peer_of(me, k, devices, n_gy):
    peer = lax.rem(me + k, devices)
    return (peer // n_gy, lax.rem(peer, n_gy))


def cell_parts(cells, half, depth):
    row = cells // depth
    short = jnp.where(cells < 0, -1, lax.rem(row, half))
    long = (row // half) * depth + lax.rem(cells, depth)
    return short.astype(jnp.float32), long.astype(jnp.float32)


def tall(row):
    return jnp.broadcast_to(row, (16, row.shape[1])).astype(BF)


def one_hot_mask(row, size):
    shape = (size // 16, 16, row.shape[1])
    index = lax.broadcasted_iota(jnp.int32, shape, 0) * 16 + lax.broadcasted_iota(jnp.int32, shape, 1)
    return index.astype(jnp.float32).astype(BF) == tall(row)[None]


def spread_block(block, cap, half, depth):
    width = block.shape[1]
    short, long = cell_parts(block[3 * cap :].astype(jnp.int32), half, depth)
    high = block[: 3 * cap].astype(BF).astype(jnp.float32)
    low = block[: 3 * cap] - high
    zero = jnp.zeros((16, width), BF)[None]
    ones = jnp.ones((16, width), BF)[None]
    lefts, rights = [], []
    for e in range(cap):
        mask = one_hot_mask(short[e : e + 1], half)
        pieces = []
        for part in (high, low):
            for c in range(3):
                value = tall(part[c * cap + e : c * cap + e + 1])
                pieces.append(jnp.where(mask, value[None], zero).reshape(half, width))
        pieces.append(jnp.where(mask, ones, zero).reshape(half, width))
        lefts.append(jnp.concatenate(pieces, axis=0))
        spot = one_hot_mask(long[e : e + 1], 2 * depth)
        rights.append(jnp.where(spot, ones, zero).reshape(2 * depth, width))
    left = jnp.concatenate(lefts, axis=1)
    right = jnp.concatenate(rights, axis=1)
    return lax.dot_general(
        left, right, (((1,), (1,)), ((), ())), preferred_element_type=jnp.float32
    )


def pick_block(table, cell_rows, cap, half, depth):
    width = cell_rows.shape[1]
    index = lax.broadcasted_iota(jnp.int32, (half, width), 0).astype(jnp.float32)
    short, long = cell_parts(cell_rows.astype(jnp.int32), half, depth)
    zero = jnp.zeros((16, width), BF)[None]
    ones = jnp.ones((16, width), BF)[None]
    rights = []
    for e in range(cap):
        spot = one_hot_mask(long[e : e + 1], 2 * depth)
        rights.append(jnp.where(spot, ones, zero).reshape(2 * depth, width))
    both = jnp.dot(table, jnp.concatenate(rights, axis=1), preferred_element_type=jnp.float32)
    rows = []
    for c in range(3):
        for e in range(cap):
            cut = both[:, e * width : (e + 1) * width]
            value = cut[c * half : (c + 1) * half] + cut[(3 + c) * half : (4 + c) * half]
            mask = index == short[e : e + 1]
            rows.append(jnp.sum(jnp.where(mask, value, 0.0), axis=0, keepdims=True))
    return jnp.concatenate(rows, axis=0)


def flow_kernel(
    n_gx, n_gy, cap, dest_ref, rank_ref, sent_ref, flow_ref, out_ref, mark_ref,
    held, acc, spread, wide, wide_force, later, table, picked, back,
    halo_send, halo_recv, block_send, block_recv, back_send, back_recv, own_sem,
):
    size_x, size_y, depth = flow_ref.shape[1:]
    half = size_x * size_y // 2
    blocks = mark_ref.shape[1]
    devices = n_gx * n_gy
    gx, gy = lax.axis_index("gx"), lax.axis_index("gy")
    me = gx * n_gy + gy

    barrier = pltpu.get_barrier_semaphore()

    def greet(k, carry):
        pl.semaphore_signal(
            barrier, inc=1, device_id=peer_of(me, k, devices, n_gy), device_id_type=MESH
        )
        return carry

    lax.fori_loop(1, devices, greet, 0)
    own = pltpu.make_async_copy(sent_ref.at[me], held.at[me], own_sem)
    own.start()
    acc[...] = jnp.zeros_like(acc)
    pl.semaphore_wait(barrier, devices - 1)

    def remote(k, src, src_at, dst, dst_at, send_sem, recv_sem):
        return pltpu.make_async_remote_copy(
            src_ref=src.at[src_at],
            dst_ref=dst.at[dst_at],
            send_sem=send_sem.at[k],
            recv_sem=recv_sem.at[k],
            device_id=peer_of(me, k, devices, n_gy),
            device_id_type=MESH,
        )

    def block_to(k):
        return remote(k, sent_ref, lax.rem(me + k, devices), held, me, block_send, block_recv)

    def block_from(k):
        sender = lax.rem(me + devices - k, devices)
        return remote(k, sent_ref, sender, held, sender, block_send, block_recv)

    def back_to(k):
        return remote(k, picked, lax.rem(me + k, devices), back, me, back_send, back_recv)

    def back_from(k):
        sender = lax.rem(me + devices - k, devices)
        return remote(k, picked, sender, back, sender, back_send, back_recv)

    def exists(dx, dy):
        x, y = gx + dx, gy + dy
        return (x >= 0) & (x < n_gx) & (y >= 0) & (y < n_gy)

    def cut(d, size, halo, room):
        if d == 0:
            return (0, size), (room, size)
        if d > 0:
            return (size - halo, halo), (room - halo, halo)
        return (0, halo), (room + size, halo)

    def side(turn, number, src, target, halo):
        dx, dy = DIRECTIONS[number]
        (sx, nx), (tx, _) = cut(dx, size_x, halo, HALO_X)
        (sy, ny), (ty, _) = cut(dy, size_y, HALO_Y, HALO_Y)
        return pltpu.make_async_remote_copy(
            src_ref=src.at[:, pl.ds(sx, nx), pl.ds(sy, ny), :],
            dst_ref=target.at[:, pl.ds(tx, nx), pl.ds(ty, ny), :],
            send_sem=halo_send.at[turn, number],
            recv_sem=halo_recv.at[turn, number],
            device_id=(gx + dx, gy + dy),
            device_id_type=MESH,
        )

    inner = (slice(HALO_X, HALO_X + size_x), slice(HALO_Y, HALO_Y + size_y))

    def sides_begin(turn, src, target, halo):
        for number, (dx, dy) in enumerate(DIRECTIONS):

            @pl.when(exists(dx, dy))
            def _():
                side(turn, number, src, target, halo).start()

            @pl.when(jnp.logical_not(exists(-dx, -dy)))
            def _():
                _, (tx, nx) = cut(dx, size_x, halo, HALO_X)
                _, (ty, ny) = cut(dy, size_y, HALO_Y, HALO_Y)
                target[:, tx : tx + nx, ty : ty + ny, :] = jnp.zeros(
                    (target.shape[0], nx, ny, depth), jnp.float32
                )

        target[:, inner[0], inner[1], :] = src[...]

    def sides_arrive(turn, src, target, halo):
        for number, (dx, dy) in enumerate(DIRECTIONS):

            @pl.when(exists(-dx, -dy))
            def _():
                side(turn, number, src, target, halo).wait_recv()

    def sides_end(turn, src, target, halo):
        for number, (dx, dy) in enumerate(DIRECTIONS):

            @pl.when(exists(dx, dy))
            def _():
                side(turn, number, src, target, halo).wait_send()

    def begin(k, carry):
        block_to(k).start()
        return carry

    lax.fori_loop(1, devices, begin, 0)
    sides_begin(0, flow_ref, wide, HALO_X)

    own.wait()
    acc[...] += spread_block(held[me], cap, half, depth)

    def gather_in(k, carry):
        block_from(k).wait_recv()
        acc[...] += spread_block(held[lax.rem(me + devices - k, devices)], cap, half, depth)
        return carry

    lax.fori_loop(1, devices, gather_in, 0)
    for c in range(4):
        if c < 3:
            total = acc[c * half : (c + 1) * half] + acc[(3 + c) * half : (4 + c) * half]
        else:
            total = acc[6 * half : 7 * half]
        spread[c, : size_x // 2] = total[:, :depth].reshape(size_x // 2, size_y, depth)
        spread[c, size_x // 2 :] = total[:, depth:].reshape(size_x // 2, size_y, depth)

    wide_x, wide_y = size_x + 2 * HALO_X, size_y + 2 * HALO_Y
    place_x = lax.broadcasted_iota(jnp.int32, (wide_x, wide_y, depth), 0) + (gx * size_x - HALO_X)
    place_y = lax.broadcasted_iota(jnp.int32, (wide_x, wide_y, depth), 1) + (gy * size_y - HALO_Y)
    keep = (
        (place_x >= 0) & (place_x < n_gx * size_x) & (place_y >= 0) & (place_y < n_gy * size_y)
    ).astype(jnp.float32)
    level = lax.broadcasted_iota(jnp.int32, (1, wide_y, depth), 2)
    not_first = (level > 0).astype(jnp.float32)
    not_last = (level < depth - 1).astype(jnp.float32)

    def up_y(v):
        return pltpu.roll(v, wide_y - 1, 1)

    def down_y(v):
        return pltpu.roll(v, 1, 1)

    def up_z(v):
        return pltpu.roll(v, depth - 1, 2) * not_last

    def down_z(v):
        return pltpu.roll(v, 1, 2) * not_first

    def around(v):
        mid = v[1:-1]
        return (v[2:] + v[:-2]) + (up_y(mid) + down_y(mid)) + (up_z(mid) + down_z(mid))

    def advance(flow, force):
        provisional = []
        for c in range(3):
            mid = flow[c][1:-1]
            stepped = mid + time_step * (viscosity * (around(flow[c]) - 6.0 * mid) + force[c])
            provisional.append(stepped * keep[1:-1])
        p0, p1, p2 = provisional
        source = (0.5 / time_step) * (
            (p0[2:] - p0[:-2])
            + (up_y(p1[1:-1]) - down_y(p1[1:-1]))
            + (up_z(p2[1:-1]) - down_z(p2[1:-1]))
        )
        sixth = keep * (1.0 / 6.0)
        pressure = -source * sixth[2:-2]
        for sweep in range(1, SWEEPS):
            edge = sweep + 2
            pressure = (around(pressure) - source[sweep:-sweep]) * sixth[edge:-edge]
        mid = pressure[1:-1]
        slopes = (
            pressure[2:] - pressure[:-2],
            up_y(mid) - down_y(mid),
            up_z(mid) - down_z(mid),
        )
        far = HALO_X - 1
        return [
            (provisional[c][far:-far] - (0.5 * time_step) * slopes[c])[:, inner[1], :] for c in range(3)
        ]

    sides_begin(1, spread, wide_force, HALO_X - 1)
    sides_arrive(0, flow_ref, wide, HALO_X)
    sides_arrive(1, spread, wide_force, HALO_X - 1)
    result = advance([wide[c] for c in range(3)], [wide_force[c, 1:-1] for c in range(3)])
    for c in range(3):
        out_ref[c] = result[c]
    for turn in range(1, STEPS):
        sides_begin(turn + 1, out_ref, later, HALO_X)
        sides_arrive(turn + 1, out_ref, later, HALO_X)
        flow = [later[c] for c in range(3)]
        force = [wide_force[c, 1:-1] - stiffness * wide_force[3, 1:-1] * flow[c][1:-1] for c in range(3)]
        result = advance(flow, force)
        sides_end(turn + 1, out_ref, later, HALO_X)
        for c in range(3):
            out_ref[c] = result[c]

    for c in range(3):
        rows = result[c].reshape(2 * half, depth)
        flat = jnp.concatenate([rows[:half], rows[half:]], axis=1)
        high = flat.astype(BF)
        table[c * half : (c + 1) * half] = high
        table[(3 + c) * half : (4 + c) * half] = (flat - high.astype(jnp.float32)).astype(BF)

    def give_back(k, carry):
        peer = lax.rem(me + k, devices)
        picked[peer] = pick_block(table[...], held[peer, 3 * cap :, :], cap, half, depth)
        back_to(k).start()
        return carry

    lax.fori_loop(1, devices, give_back, 0)
    back[me] = pick_block(table[...], held[me, 3 * cap :, :], cap, half, depth)

    def finish(k, carry):
        block_to(k).wait_send()
        back_from(k).wait_recv()
        return carry

    lax.fori_loop(1, devices, finish, 0)

    def take(b, carry):
        dest = dest_ref[b]
        rank = rank_ref[b]
        for c in range(3):
            mark_ref[c, pl.ds(b, 1), :] = back[dest, pl.ds(c * cap + rank, 1), :]
        return carry

    lax.fori_loop(0, blocks, take, 0, unroll=4)

    def drain(k, carry):
        back_to(k).wait_send()
        return carry

    lax.fori_loop(1, devices, drain, 0)
    sides_end(0, flow_ref, wide, HALO_X)
    sides_end(1, spread, wide_force, HALO_X - 1)


def body(n_gx, n_gy, velocity, marker_force, marker_cell, block_brick):
    devices = n_gx * n_gy
    blocks, width = marker_cell.shape
    size_x, size_y, depth = velocity.shape[1:]
    cap = 2 * blocks // devices
    rows = size_x * size_y
    half = rows // 2
    sent, dest, rank = pl.pallas_call(
        functools.partial(pack_kernel, devices, cap),
        out_shape=(
            jax.ShapeDtypeStruct((devices, 4 * cap, width), jnp.float32),
            jax.ShapeDtypeStruct((blocks,), jnp.int32),
            jax.ShapeDtypeStruct((blocks,), jnp.int32),
        ),
        in_specs=[SMEM, VMEM, VMEM],
        out_specs=(VMEM, SMEM, SMEM),
        scratch_shapes=[pltpu.SMEM((devices,), jnp.int32)],
    )(block_brick.reshape(blocks), marker_force, marker_cell)
    wide = (size_x + 2 * HALO_X, size_y + 2 * HALO_Y, depth)
    many = pltpu.SemaphoreType.DMA((devices,))
    return pl.pallas_call(
        functools.partial(flow_kernel, n_gx, n_gy, cap),
        out_shape=(
            jax.ShapeDtypeStruct(velocity.shape, jnp.float32),
            jax.ShapeDtypeStruct((3, blocks, width), jnp.float32),
        ),
        in_specs=[SMEM, SMEM, VMEM, VMEM],
        out_specs=(VMEM, VMEM),
        scratch_shapes=[
            pltpu.VMEM(sent.shape, jnp.float32),
            pltpu.VMEM((7 * half, 2 * depth), jnp.float32),
            pltpu.VMEM((4, size_x, size_y, depth), jnp.float32),
            pltpu.VMEM((3,) + wide, jnp.float32),
            pltpu.VMEM((4,) + wide, jnp.float32),
            pltpu.VMEM((3,) + wide, jnp.float32),
            pltpu.VMEM((6 * half, 2 * depth), BF),
            pltpu.VMEM((devices, 3 * cap, width), jnp.float32),
            pltpu.VMEM((devices, 3 * cap, width), jnp.float32),
            pltpu.SemaphoreType.DMA((STEPS + 1, 8)),
            pltpu.SemaphoreType.DMA((STEPS + 1, 8)),
            many,
            many,
            many,
            many,
            pltpu.SemaphoreType.DMA,
        ],
        compiler_params=pltpu.CompilerParams(
            collective_id=0, has_side_effects=True, vmem_limit_bytes=40 << 20
        ),
    )(dest, rank, sent, velocity)


def solution(mesh):
    n_gx, n_gy = mesh.shape["gx"], mesh.shape["gy"]
    return jax.shard_map(
        functools.partial(body, n_gx, n_gy),
        mesh=mesh,
        in_specs=(
            P(None, "gx", "gy", None),
            P(None, ("gx", "gy"), None),
            P(("gx", "gy"), None),
            P(("gx", "gy"), None),
        ),
        out_specs=(P(None, "gx", "gy", None), P(None, ("gx", "gy"), None)),
        check_vma=False,
    )
```

```python
import functools

import jax
import jax.numpy as jnp
from jax import lax
from jax.experimental import pallas as pl
from jax.experimental.pallas import tpu as pltpu
from jax.sharding import PartitionSpec as P

SWEEPS = 4
STEPS = 2
MESH = pl.DeviceIdType.MESH

time_step = 0.5
viscosity = 0.2
stiffness = 1.0

HALO_X = SWEEPS + 2
HALO_Y = 8

BF = jnp.bfloat16
VMEM = pl.BlockSpec(memory_space=pltpu.VMEM)
SMEM = pl.BlockSpec(memory_space=pltpu.SMEM)
DIRECTIONS = [(i, j) for i in (-1, 0, 1) for j in (-1, 0, 1) if (i, j) != (0, 0)]


def pack_kernel(devices, cap, brick_ref, force_ref, cell_ref, out_ref, dest_ref, rank_ref, seen):
    blocks, width = cell_ref.shape
    out_ref[:, : 3 * cap, :] = jnp.zeros((devices, 3 * cap, width), jnp.float32)
    out_ref[:, 3 * cap :, :] = jnp.full((devices, cap, width), -1.0, jnp.float32)

    def clear(i, carry):
        seen[i] = 0
        return carry

    lax.fori_loop(0, devices, clear, 0)

    def place(b, carry):
        dest = brick_ref[b]
        rank = seen[dest]
        seen[dest] = rank + 1
        dest_ref[b] = dest
        rank_ref[b] = rank
        for c in range(3):
            out_ref[dest, pl.ds(c * cap + rank, 1), :] = force_ref[c, pl.ds(b, 1), :]
        out_ref[dest, pl.ds(3 * cap + rank, 1), :] = cell_ref[pl.ds(b, 1), :].astype(jnp.float32)
        return carry

    lax.fori_loop(0, blocks, place, 0, unroll=4)


def peer_of(me, k, devices, n_gy):
    peer = lax.rem(me + k, devices)
    return (peer // n_gy, lax.rem(peer, n_gy))


def cell_parts(cells, half, depth):
    row = cells // depth
    short = jnp.where(cells < 0, -1, lax.rem(row, half))
    long = (row // half) * depth + lax.rem(cells, depth)
    return short.astype(jnp.float32), long.astype(jnp.float32)


def tall(row):
    return jnp.broadcast_to(row, (16, row.shape[1])).astype(BF)


def one_hot_mask(row, size):
    shape = (size // 16, 16, row.shape[1])
    index = lax.broadcasted_iota(jnp.int32, shape, 0) * 16 + lax.broadcasted_iota(jnp.int32, shape, 1)
    return index.astype(jnp.float32).astype(BF) == tall(row)[None]


def spread_block(block, cap, half, depth):
    width = block.shape[1]
    short, long = cell_parts(block[3 * cap :].astype(jnp.int32), half, depth)
    high = block[: 3 * cap].astype(BF).astype(jnp.float32)
    low = block[: 3 * cap] - high
    zero = jnp.zeros((16, width), BF)[None]
    ones = jnp.ones((16, width), BF)[None]
    lefts, rights = [], []
    for e in range(cap):
        mask = one_hot_mask(short[e : e + 1], half)
        pieces = []
        for part in (high, low):
            for c in range(3):
                value = tall(part[c * cap + e : c * cap + e + 1])
                pieces.append(jnp.where(mask, value[None], zero).reshape(half, width))
        pieces.append(jnp.where(mask, ones, zero).reshape(half, width))
        lefts.append(jnp.concatenate(pieces, axis=0))
        spot = one_hot_mask(long[e : e + 1], 2 * depth)
        rights.append(jnp.where(spot, ones, zero).reshape(2 * depth, width))
    left = jnp.concatenate(lefts, axis=1)
    right = jnp.concatenate(rights, axis=1)
    return lax.dot_general(
        left, right, (((1,), (1,)), ((), ())), preferred_element_type=jnp.float32
    )


def pick_block(table, cell_rows, cap, half, depth):
    width = cell_rows.shape[1]
    index = lax.broadcasted_iota(jnp.int32, (half, width), 0).astype(jnp.float32)
    short, long = cell_parts(cell_rows.astype(jnp.int32), half, depth)
    zero = jnp.zeros((16, width), BF)[None]
    ones = jnp.ones((16, width), BF)[None]
    rights = []
    for e in range(cap):
        spot = one_hot_mask(long[e : e + 1], 2 * depth)
        rights.append(jnp.where(spot, ones, zero).reshape(2 * depth, width))
    both = jnp.dot(table, jnp.concatenate(rights, axis=1), preferred_element_type=jnp.float32)
    rows = []
    for c in range(3):
        for e in range(cap):
            cut = both[:, e * width : (e + 1) * width]
            value = cut[c * half : (c + 1) * half] + cut[(3 + c) * half : (4 + c) * half]
            mask = index == short[e : e + 1]
            rows.append(jnp.sum(jnp.where(mask, value, 0.0), axis=0, keepdims=True))
    return jnp.concatenate(rows, axis=0)


def flow_kernel(
    n_gx, n_gy, cap, dest_ref, rank_ref, sent_ref, flow_ref, out_ref, mark_ref,
    held, acc, spread, wide, wide_force, later, table, picked, back, corner_out, corner_in,
    halo_send, halo_recv, block_send, block_recv, back_send, back_recv, own_sem,
):
    size_x, size_y, depth = flow_ref.shape[1:]
    half = size_x * size_y // 2
    blocks = mark_ref.shape[1]
    devices = n_gx * n_gy
    gx, gy = lax.axis_index("gx"), lax.axis_index("gy")
    me = gx * n_gy + gy

    barrier = pltpu.get_barrier_semaphore()

    def greet(k, carry):
        pl.semaphore_signal(
            barrier, inc=1, device_id=peer_of(me, k, devices, n_gy), device_id_type=MESH
        )
        return carry

    lax.fori_loop(1, devices, greet, 0)
    own = pltpu.make_async_copy(sent_ref.at[me], held.at[me], own_sem)
    own.start()
    acc[...] = jnp.zeros_like(acc)
    pl.semaphore_wait(barrier, devices - 1)

    def remote(k, src, src_at, dst, dst_at, send_sem, recv_sem):
        return pltpu.make_async_remote_copy(
            src_ref=src.at[src_at],
            dst_ref=dst.at[dst_at],
            send_sem=send_sem.at[k],
            recv_sem=recv_sem.at[k],
            device_id=peer_of(me, k, devices, n_gy),
            device_id_type=MESH,
        )

    def block_to(k):
        return remote(k, sent_ref, lax.rem(me + k, devices), held, me, block_send, block_recv)

    def block_from(k):
        sender = lax.rem(me + devices - k, devices)
        return remote(k, sent_ref, sender, held, sender, block_send, block_recv)

    def back_to(k):
        return remote(k, picked, lax.rem(me + k, devices), back, me, back_send, back_recv)

    def back_from(k):
        sender = lax.rem(me + devices - k, devices)
        return remote(k, picked, sender, back, sender, back_send, back_recv)

    def exists(dx, dy):
        x, y = gx + dx, gy + dy
        return (x >= 0) & (x < n_gx) & (y >= 0) & (y < n_gy)

    def cut(d, size, halo, room):
        if d == 0:
            return (0, size), (room, size)
        if d > 0:
            return (size - halo, halo), (room - halo, halo)
        return (0, halo), (room + size, halo)

    def triangle(halo):
        rows, first = [], 0
        for i in range(1, halo):
            rows.append((i, first, halo - i))
            first += halo - i
        return rows

    def side(turn, number, src, target, halo):
        dx, dy = DIRECTIONS[number]
        if dx and dy:
            fields = src.shape[0]
            return pltpu.make_async_remote_copy(
                src_ref=corner_out.at[turn, number, pl.ds(0, fields)],
                dst_ref=corner_in.at[turn, number, pl.ds(0, fields)],
                send_sem=halo_send.at[turn, number],
                recv_sem=halo_recv.at[turn, number],
                device_id=(gx + dx, gy + dy),
                device_id_type=MESH,
            )
        (sx, nx), (tx, _) = cut(dx, size_x, halo, HALO_X)
        (sy, ny), (ty, _) = cut(dy, size_y, HALO_Y, HALO_Y)
        return pltpu.make_async_remote_copy(
            src_ref=src.at[:, pl.ds(sx, nx), pl.ds(sy, ny), :],
            dst_ref=target.at[:, pl.ds(tx, nx), pl.ds(ty, ny), :],
            send_sem=halo_send.at[turn, number],
            recv_sem=halo_recv.at[turn, number],
            device_id=(gx + dx, gy + dy),
            device_id_type=MESH,
        )

    def fill_corner(turn, number, src, halo):
        dx, dy = DIRECTIONS[number]
        fields = src.shape[0]
        for i, first, n in triangle(halo):
            x = size_x - i if dx > 0 else i - 1
            y = size_y - n if dy > 0 else 0
            corner_out[turn, number, :fields, first : first + n, :] = src[:, x, y : y + n, :]

    def place_corner(turn, number, target, halo):
        dx, dy = DIRECTIONS[number]
        fields = target.shape[0]
        for i, first, n in triangle(halo):
            x = HALO_X - i if dx > 0 else HALO_X + size_x + i - 1
            y = HALO_Y - n if dy > 0 else HALO_Y + size_y
            target[:, x, y : y + n, :] = corner_in[turn, number, :fields, first : first + n, :]

    inner = (slice(HALO_X, HALO_X + size_x), slice(HALO_Y, HALO_Y + size_y))

    def sides_begin(turn, src, target, halo):
        for number, (dx, dy) in enumerate(DIRECTIONS):
            if not (dx and dy):

                @pl.when(exists(dx, dy))
                def _():
                    side(turn, number, src, target, halo).start()

        for number, (dx, dy) in enumerate(DIRECTIONS):
            if dx and dy:
                fill_corner(turn, number, src, halo)

                @pl.when(exists(dx, dy))
                def _():
                    side(turn, number, src, target, halo).start()

                _, (tx, nx) = cut(dx, size_x, halo, HALO_X)
                _, (ty, ny) = cut(dy, size_y, HALO_Y, HALO_Y)
                target[:, tx : tx + nx, ty : ty + ny, :] = jnp.zeros(
                    (target.shape[0], nx, ny, depth), jnp.float32
                )
            else:

                @pl.when(jnp.logical_not(exists(-dx, -dy)))
                def _():
                    _, (tx, nx) = cut(dx, size_x, halo, HALO_X)
                    _, (ty, ny) = cut(dy, size_y, HALO_Y, HALO_Y)
                    target[:, tx : tx + nx, ty : ty + ny, :] = jnp.zeros(
                        (target.shape[0], nx, ny, depth), jnp.float32
                    )

        target[:, inner[0], inner[1], :] = src[...]

    def sides_arrive(turn, src, target, halo):
        for number, (dx, dy) in enumerate(DIRECTIONS):

            @pl.when(exists(-dx, -dy))
            def _():
                side(turn, number, src, target, halo).wait_recv()
                if dx and dy:
                    place_corner(turn, number, target, halo)

    def sides_end(turn, src, target, halo):
        for number, (dx, dy) in enumerate(DIRECTIONS):

            @pl.when(exists(dx, dy))
            def _():
                side(turn, number, src, target, halo).wait_send()

    def begin(k, carry):
        block_to(k).start()
        return carry

    lax.fori_loop(1, devices, begin, 0)
    sides_begin(0, flow_ref, wide, HALO_X)

    own.wait()
    acc[...] += spread_block(held[me], cap, half, depth)

    def gather_in(k, carry):
        block_from(k).wait_recv()
        acc[...] += spread_block(held[lax.rem(me + devices - k, devices)], cap, half, depth)
        return carry

    lax.fori_loop(1, devices, gather_in, 0)
    for c in range(4):
        if c < 3:
            total = acc[c * half : (c + 1) * half] + acc[(3 + c) * half : (4 + c) * half]
        else:
            total = acc[6 * half : 7 * half]
        spread[c, : size_x // 2] = total[:, :depth].reshape(size_x // 2, size_y, depth)
        spread[c, size_x // 2 :] = total[:, depth:].reshape(size_x // 2, size_y, depth)

    wide_x, wide_y = size_x + 2 * HALO_X, size_y + 2 * HALO_Y
    place_x = lax.broadcasted_iota(jnp.int32, (wide_x, wide_y, depth), 0) + (gx * size_x - HALO_X)
    place_y = lax.broadcasted_iota(jnp.int32, (wide_x, wide_y, depth), 1) + (gy * size_y - HALO_Y)
    keep = (
        (place_x >= 0) & (place_x < n_gx * size_x) & (place_y >= 0) & (place_y < n_gy * size_y)
    ).astype(jnp.float32)
    level = lax.broadcasted_iota(jnp.int32, (1, wide_y, depth), 2)
    not_first = (level > 0).astype(jnp.float32)
    not_last = (level < depth - 1).astype(jnp.float32)

    def up_y(v):
        return pltpu.roll(v, wide_y - 1, 1)

    def down_y(v):
        return pltpu.roll(v, 1, 1)

    def up_z(v):
        return pltpu.roll(v, depth - 1, 2) * not_last

    def down_z(v):
        return pltpu.roll(v, 1, 2) * not_first

    def around(v):
        mid = v[1:-1]
        return (v[2:] + v[:-2]) + (up_y(mid) + down_y(mid)) + (up_z(mid) + down_z(mid))

    def advance(flow, force):
        provisional = []
        for c in range(3):
            mid = flow[c][1:-1]
            stepped = mid + time_step * (viscosity * (around(flow[c]) - 6.0 * mid) + force[c])
            provisional.append(stepped * keep[1:-1])
        p0, p1, p2 = provisional
        source = (0.5 / time_step) * (
            (p0[2:] - p0[:-2])
            + (up_y(p1[1:-1]) - down_y(p1[1:-1]))
            + (up_z(p2[1:-1]) - down_z(p2[1:-1]))
        )
        sixth = keep * (1.0 / 6.0)
        pressure = -source * sixth[2:-2]
        for sweep in range(1, SWEEPS):
            edge = sweep + 2
            pressure = (around(pressure) - source[sweep:-sweep]) * sixth[edge:-edge]
        mid = pressure[1:-1]
        slopes = (
            pressure[2:] - pressure[:-2],
            up_y(mid) - down_y(mid),
            up_z(mid) - down_z(mid),
        )
        far = HALO_X - 1
        return [
            (provisional[c][far:-far] - (0.5 * time_step) * slopes[c])[:, inner[1], :] for c in range(3)
        ]

    sides_begin(1, spread, wide_force, HALO_X - 1)
    sides_arrive(0, flow_ref, wide, HALO_X)
    sides_arrive(1, spread, wide_force, HALO_X - 1)
    result = advance([wide[c] for c in range(3)], [wide_force[c, 1:-1] for c in range(3)])
    for c in range(3):
        out_ref[c] = result[c]
    for turn in range(1, STEPS):
        sides_begin(turn + 1, out_ref, later, HALO_X)
        sides_arrive(turn + 1, out_ref, later, HALO_X)
        flow = [later[c] for c in range(3)]
        force = [wide_force[c, 1:-1] - stiffness * wide_force[3, 1:-1] * flow[c][1:-1] for c in range(3)]
        result = advance(flow, force)
        sides_end(turn + 1, out_ref, later, HALO_X)
        for c in range(3):
            out_ref[c] = result[c]

    for c in range(3):
        rows = result[c].reshape(2 * half, depth)
        flat = jnp.concatenate([rows[:half], rows[half:]], axis=1)
        high = flat.astype(BF)
        table[c * half : (c + 1) * half] = high
        table[(3 + c) * half : (4 + c) * half] = (flat - high.astype(jnp.float32)).astype(BF)

    def give_back(k, carry):
        peer = lax.rem(me + k, devices)
        picked[peer] = pick_block(table[...], held[peer, 3 * cap :, :], cap, half, depth)
        back_to(k).start()
        return carry

    lax.fori_loop(1, devices, give_back, 0)
    back[me] = pick_block(table[...], held[me, 3 * cap :, :], cap, half, depth)

    def finish(k, carry):
        block_to(k).wait_send()
        back_from(k).wait_recv()
        return carry

    lax.fori_loop(1, devices, finish, 0)

    def take(b, carry):
        dest = dest_ref[b]
        rank = rank_ref[b]
        for c in range(3):
            mark_ref[c, pl.ds(b, 1), :] = back[dest, pl.ds(c * cap + rank, 1), :]
        return carry

    lax.fori_loop(0, blocks, take, 0, unroll=4)

    def drain(k, carry):
        back_to(k).wait_send()
        return carry

    lax.fori_loop(1, devices, drain, 0)
    sides_end(0, flow_ref, wide, HALO_X)
    sides_end(1, spread, wide_force, HALO_X - 1)


def body(n_gx, n_gy, velocity, marker_force, marker_cell, block_brick):
    devices = n_gx * n_gy
    blocks, width = marker_cell.shape
    size_x, size_y, depth = velocity.shape[1:]
    cap = 2 * blocks // devices
    rows = size_x * size_y
    half = rows // 2
    sent, dest, rank = pl.pallas_call(
        functools.partial(pack_kernel, devices, cap),
        out_shape=(
            jax.ShapeDtypeStruct((devices, 4 * cap, width), jnp.float32),
            jax.ShapeDtypeStruct((blocks,), jnp.int32),
            jax.ShapeDtypeStruct((blocks,), jnp.int32),
        ),
        in_specs=[SMEM, VMEM, VMEM],
        out_specs=(VMEM, SMEM, SMEM),
        scratch_shapes=[pltpu.SMEM((devices,), jnp.int32)],
    )(block_brick.reshape(blocks), marker_force, marker_cell)
    wide = (size_x + 2 * HALO_X, size_y + 2 * HALO_Y, depth)
    many = pltpu.SemaphoreType.DMA((devices,))
    return pl.pallas_call(
        functools.partial(flow_kernel, n_gx, n_gy, cap),
        out_shape=(
            jax.ShapeDtypeStruct(velocity.shape, jnp.float32),
            jax.ShapeDtypeStruct((3, blocks, width), jnp.float32),
        ),
        in_specs=[SMEM, SMEM, VMEM, VMEM],
        out_specs=(VMEM, VMEM),
        scratch_shapes=[
            pltpu.VMEM(sent.shape, jnp.float32),
            pltpu.VMEM((7 * half, 2 * depth), jnp.float32),
            pltpu.VMEM((4, size_x, size_y, depth), jnp.float32),
            pltpu.VMEM((3,) + wide, jnp.float32),
            pltpu.VMEM((4,) + wide, jnp.float32),
            pltpu.VMEM((3,) + wide, jnp.float32),
            pltpu.VMEM((6 * half, 2 * depth), BF),
            pltpu.VMEM((devices, 3 * cap, width), jnp.float32),
            pltpu.VMEM((devices, 3 * cap, width), jnp.float32),
            pltpu.VMEM((STEPS + 1, 8, 4, 16, depth), jnp.float32),
            pltpu.VMEM((STEPS + 1, 8, 4, 16, depth), jnp.float32),
            pltpu.SemaphoreType.DMA((STEPS + 1, 8)),
            pltpu.SemaphoreType.DMA((STEPS + 1, 8)),
            many,
            many,
            many,
            many,
            pltpu.SemaphoreType.DMA,
        ],
        compiler_params=pltpu.CompilerParams(
            collective_id=0, has_side_effects=True, vmem_limit_bytes=40 << 20
        ),
    )(dest, rank, sent, velocity)


def solution(mesh):
    n_gx, n_gy = mesh.shape["gx"], mesh.shape["gy"]
    return jax.shard_map(
        functools.partial(body, n_gx, n_gy),
        mesh=mesh,
        in_specs=(
            P(None, "gx", "gy", None),
            P(None, ("gx", "gy"), None),
            P(("gx", "gy"), None),
            P(("gx", "gy"), None),
        ),
        out_specs=(P(None, "gx", "gy", None), P(None, ("gx", "gy"), None)),
        check_vma=False,
    )
```
